256 devices in a mesh: dp: 8 (over z_hi, core), seq: 32 (over x, z_lo, y).
Axes of the slice: x: 4, y: 4, z: 8 (z_hi: 4, z_lo: 2; z = z_hi * 2 + z_lo), core: 2. Of those that a mesh axis runs over, the one named last changes fastest.
Arguments:
- normed: bfloat16 [8, 8192, 512], P('dp', 'seq'), may hold values from -6 to 6
- query_states: bfloat16 [8, 8192, 512], P('dp', 'seq'), may hold values from -6 to 6
- key_states: bfloat16 [8, 8192, 512], P('dp', 'seq'), may hold values from -6 to 6
- value_states: bfloat16 [8, 8192, 512], P('dp', 'seq'), may hold values from -6 to 6
- grad_output: bfloat16 [8, 8192, 512], P('dp', 'seq'), may hold values from -6 to 6
- w_qkv: bfloat16 [512, 1536], replicated, may hold values from -0.25 to 0.25
- w_out: bfloat16 [512, 512], replicated, may hold values from -0.25 to 0.25
- scene_tiles: int32 [8, 32], P('dp'), may hold values from 1 to 64, 256 in all within a row
Outputs:
- grad_normed: bfloat16 [8, 8192, 512], P('dp', 'seq')
- grad_w_qkv: float32 [512, 1536], replicated
- grad_w_out: float32 [512, 512], replicated
The draws below stay inside these ranges and needn't reach their ends.
Inputs may be any that keep to these rules, and one draw needn't show every extreme that they name: `scene_tiles`: each row sums to 256; the largest entry of each row is exactly 64.
All inputs are finite; a program needn't handle non-finite values.
Results may differ from the reference program's by a relative error of at most 0.025.
Values may be sent and summed in bfloat16 or wider, within the bound.
No kernel may reach another device: no remote copies, remote signals or barrier semaphores. Data moves between devices by JAX's collectives and lax.ppermute only.
A program may use at most 128 MiB of HBM per device.

```python
import math
import jax
import jax.numpy as jnp
import numpy as np
from jax import lax

D = 512
HEADS = 8
TILE = 32
MAXLEN = 2048
TOK_DEV = 256
REACH = 8
TOKENS = 8192
SCENES = 32
N_DP = 8
N_SEQ = 32


def draw_query_states(key, part):
    key = jax.random.fold_in(key, 5)
    drawn = jnp.clip(jax.random.normal(key, (N_DP, TOKENS, D), jnp.float32), -5.0, 5.0)
    return drawn.astype(jnp.bfloat16)


def draw_key_states(key, part):
    key = jax.random.fold_in(key, 7)
    drawn = jnp.clip(jax.random.normal(key, (N_DP, TOKENS, D), jnp.float32), -5.0, 5.0)
    return drawn.astype(jnp.bfloat16)


def steps_of(key, shape, split, least, largest):
    loudness = 1.0
    for dim, parts in split:
        draws = jax.random.uniform(jax.random.fold_in(jax.random.fold_in(key, 6), dim), (parts,), jnp.float32, least / len(split), largest / len(split))
        loudness = loudness * jnp.repeat(jnp.exp(draws), shape[dim] // parts).reshape((-1,) + (1,) * (len(shape) - 1 - dim))
    return loudness


def profile(amount, total, bound, skew):
    weights = [(1 << 20) // math.isqrt(rank ** skew) + 1 for rank in range(2, amount + 1)]
    surplus, counts = total - bound - (amount - 1), [1] * (amount - 1)
    while surplus > 0:
        movable = [i for i in range(amount - 1) if counts[i] < bound]
        mass, budget = sum([weights[i] for i in movable]), surplus
        for i in movable:
            extra = min(bound - counts[i], max(1, budget * weights[i] // mass), surplus)
            counts[i] = counts[i] + extra
            surplus = surplus - extra
    return np.array([bound] + counts)


def ragged(stream_key, amount, total, most, lean):
    if amount == 2:
        one = jax.random.randint(stream_key, (), max(1, total - most), min(most, total - 1) + 1)
        return jnp.stack([one, total - one])
    sizes = jnp.asarray(profile(amount, total, most, lean), jnp.int32)
    couples = (amount - 1) // 2
    donor, taker = sizes[1:1 + 2 * couples:2], sizes[2:2 + 2 * couples:2]
    margin = jnp.minimum(donor - 1, most - taker)
    moved = jax.random.randint(jax.random.fold_in(stream_key, 1), (couples,), 0, 1 << 20) % (margin + 1)
    sizes = sizes.at[1:1 + 2 * couples:2].set(donor - moved).at[2:2 + 2 * couples:2].set(taker + moved)
    return sizes[jax.random.permutation(jax.random.fold_in(stream_key, 2), amount)]


def normal_values(rng, extent, deviation, limit, cuts=(), held_as=jnp.bfloat16):
    result = jax.random.normal(rng, extent, jnp.float32) * deviation
    if len(cuts) > 0:
        result = steps_of(rng, extent, cuts, -0.22, 0.18) * result
    return jnp.clip(result, min=-limit, max=limit).astype(held_as)


def setup_inputs(seed: int = 0) -> dict:
    key_of = jax.random.split(jax.random.key(seed), 9)
    return {
        "normed": normal_values(key_of[0], (N_DP, TOKENS, D), 1.0, 6.0, ((0, 8), (1, 32))),
        "query_states": draw_query_states(jax.random.fold_in(key_of[8], 71), 0),
        "key_states": draw_key_states(jax.random.fold_in(key_of[8], 71), 0),
        "value_states": normal_values(key_of[3], (N_DP, TOKENS, D), 1.0, 6.0, ((0, 8), (1, 32))),
        "grad_output": normal_values(key_of[4], (N_DP, TOKENS, D), 0.5, 6.0, ((0, 8), (1, 32))),
        "w_qkv": normal_values(key_of[5], (D, 3 * D), D ** -0.5, 0.25),
        "w_out": normal_values(key_of[6], (D, D), D ** -0.5, 0.25),
        "scene_tiles": jax.vmap(lambda own: ragged(own, SCENES, TOKENS // TILE, MAXLEN // TILE, 2))(jax.random.split(key_of[7], N_DP)).reshape((N_DP, SCENES)).astype(jnp.int32),
    }


def batched(form, left, right):
    return jnp.einsum(form, left.astype(jnp.float32), right.astype(jnp.float32))


def scene_of(scene_ends, positions):
    passed = (scene_ends[None, :] <= positions[:, None]).astype(jnp.int32)
    return jnp.sum(passed, axis=1).astype(jnp.int32)


def piece_mask(scene_ends, query_scene, device, device_count, tok_rows):
    inside = jnp.logical_and(device >= 0, device < device_count)
    key_scene = scene_of(scene_ends, device * tok_rows + jnp.arange(tok_rows, dtype=jnp.int32))
    allowed = jnp.logical_and(inside, query_scene[:, None] == key_scene[None, :])
    intersection = jnp.logical_and(key_scene[0] <= query_scene[-1], key_scene[-1] >= query_scene[0])
    return allowed, jnp.logical_and(inside, intersection)


def block_grads(query3, grad_rows, w_out, window, first_device, device_count, scene_ends, query_scene):
    tok_rows, head_count, head_size = query3.shape
    model_width = head_count * head_size
    score_scale = head_size ** -0.5
    piece_total = window.shape[0]

    def scores_of(piece):
        key3 = window[piece, 0].reshape(tok_rows, head_count, head_size)
        return batched("qhe,khe->hqk", query3, key3) * score_scale

    def geometry(piece):
        return piece_mask(scene_ends, query_scene, first_device + piece, device_count, tok_rows)

    def first_step(piece, carry_in):
        piece = jnp.asarray(piece).astype(jnp.int32)
        allowed, shared = geometry(piece)

        def update(carried):
            old_max, old_sum, accum = carried
            masked = jnp.where(allowed[None], scores_of(piece), -1e30)
            tile_max = jnp.max(masked, axis=2)
            exp_terms = jnp.where(allowed[None], jnp.exp(masked - tile_max[:, :, None]), 0.0)
            tile_sum = jnp.sum(exp_terms, axis=2)
            value3 = window[piece, 1].reshape(tok_rows, head_count, head_size)
            partial_value = batched("hqk,khe->qhe", exp_terms.astype(jnp.bfloat16), value3)
            new_max = jnp.maximum(old_max, tile_max)
            old_factor = jnp.exp(old_max - new_max)
            tile_factor = jnp.exp(tile_max - new_max)
            new_sum = old_sum * old_factor + tile_sum * tile_factor
            new_accum = accum * old_factor.T[:, :, None] + partial_value * tile_factor.T[:, :, None]
            return new_max, new_sum, new_accum

        return lax.cond(shared, update, lambda carried: carried, carry_in)

    start_max = jnp.full((head_count, tok_rows), -1e30, jnp.float32)
    start_sum = jnp.zeros((head_count, tok_rows), jnp.float32)
    start_accum = jnp.zeros((tok_rows, head_count, head_size), jnp.float32)
    run_max, run_sum, out_sum = lax.fori_loop(0, piece_total, first_step, (start_max, start_sum, start_accum))

    def probs_of(piece, allowed):
        shifted = jnp.exp(scores_of(piece) - run_max[:, :, None]) / run_sum[:, :, None]
        return jnp.where(allowed[None], shifted, 0.0)

    attended = (out_sum / run_sum.T[:, :, None]).astype(jnp.bfloat16).reshape(tok_rows, model_width)
    grad_att = jnp.dot(grad_rows, w_out.T, preferred_element_type=jnp.float32).astype(jnp.bfloat16)
    grad3 = grad_att.reshape(tok_rows, head_count, head_size)
    att3 = attended.reshape(tok_rows, head_count, head_size)
    row_dots = jnp.sum(grad3.astype(jnp.float32) * att3.astype(jnp.float32), axis=2).T

    def grad_step(accum, piece):
        allowed, shared = geometry(piece)

        def update(carried):
            softmax_rows = probs_of(piece, allowed)
            weights = softmax_rows.astype(jnp.bfloat16)
            key3 = window[piece, 0].reshape(tok_rows, head_count, head_size)
            value3 = window[piece, 1].reshape(tok_rows, head_count, head_size)
            grad_probs = batched("qhe,khe->hqk", grad3, value3)
            grad_scores = (softmax_rows * (grad_probs - row_dots[:, :, None]) * score_scale).astype(jnp.bfloat16)
            new_carried = carried + batched("hqk,khe->qhe", grad_scores, key3)
            grad_keys = batched("hqk,qhe->khe", grad_scores, query3).astype(jnp.bfloat16).reshape(tok_rows, model_width)
            grad_values = batched("hqk,qhe->khe", weights, grad3).astype(jnp.bfloat16).reshape(tok_rows, model_width)
            return new_carried, jnp.stack([grad_keys, grad_values])

        def passby(carried):
            return carried, jnp.zeros((2, tok_rows, model_width), jnp.bfloat16)

        return lax.cond(shared, update, passby, accum)

    grad_sum, grad_terms = lax.scan(grad_step, jnp.zeros((tok_rows, head_count, head_size), jnp.float32),
                                    jnp.arange(piece_total, dtype=jnp.int32))
    return grad_sum.astype(jnp.bfloat16).reshape(tok_rows, model_width), attended, grad_terms


def reference(normed, query_states, key_states, value_states, grad_output, w_qkv, w_out, scene_tiles):
    window_size = 2 * REACH + 1

    def one_group(members):
        normed_g, query_g, key_g, value_g, grad_g, tiles_g = members
        scene_ends = (jnp.cumsum(tiles_g) * TILE).astype(jnp.int32)
        paired = jnp.stack([key_g, value_g]).reshape(2, N_SEQ, TOK_DEV, D).transpose(1, 0, 2, 3)
        padded = jnp.pad(paired, ((REACH, REACH), (0, 0), (0, 0), (0, 0)))
        query_blocks = query_g.reshape(N_SEQ, TOK_DEV, HEADS, D // HEADS)
        grad_blocks = grad_g.reshape(N_SEQ, TOK_DEV, D)

        def block_step(carried, block):
            window = lax.dynamic_slice_in_dim(padded, block, window_size, 0)
            positions = block * TOK_DEV + jnp.arange(TOK_DEV, dtype=jnp.int32)
            query_scene = scene_of(scene_ends, positions)
            grad_query, attended, grad_terms = block_grads(query_blocks[block], grad_blocks[block], w_out, window,
                                                           block - REACH, N_SEQ, scene_ends, query_scene)
            current = lax.dynamic_slice_in_dim(carried, block, window_size, 0)
            carried = lax.dynamic_update_slice_in_dim(carried, current + grad_terms.astype(jnp.float32), block, 0)
            return carried, (grad_query, attended)

        start = jnp.zeros((N_SEQ + 2 * REACH, 2, TOK_DEV, D), jnp.float32)
        summed, (grad_query, attended) = lax.scan(block_step, start, jnp.arange(N_SEQ, dtype=jnp.int32))
        grad_pairs = summed[REACH:REACH + N_SEQ].astype(jnp.bfloat16)
        grad_qkv = jnp.concatenate([grad_query.reshape(TOKENS, D), grad_pairs[:, 0].reshape(TOKENS, D),
                                    grad_pairs[:, 1].reshape(TOKENS, D)], axis=1)
        w_grad_qkv = jnp.dot(normed_g.T, grad_qkv, preferred_element_type=jnp.float32)
        w_grad_out = jnp.dot(attended.reshape(TOKENS, D).T, grad_g, preferred_element_type=jnp.float32)
        grad_in = jnp.dot(grad_qkv, w_qkv.T, preferred_element_type=jnp.float32).astype(jnp.bfloat16)
        return grad_in, w_grad_qkv, w_grad_out

    grad_normed, qkv_parts, out_parts = lax.map(one_group, (normed, query_states, key_states, value_states,
                                                            grad_output, scene_tiles))
    return grad_normed, jnp.sum(qkv_parts, axis=0), jnp.sum(out_parts, axis=0)
```

```python
import jax
import jax.numpy as jnp
from jax import lax
from jax.experimental import pallas as pl
from jax.experimental.pallas import tpu as pltpu
from jax.sharding import Mesh
from jax.sharding import PartitionSpec as P

HEADS = 8
HEAD = 64
TILE = 32
TOK = 256
SCENES = 32
BARRED = 16384.0
F32 = jnp.float32
BF16 = jnp.bfloat16
NT = (((1,), (1,)), ((), ()))
TN = (((0,), (0,)), ((), ()))
VMEM_LIMIT = 48 * 1024 * 1024


def params():
    return pltpu.CompilerParams(vmem_limit_bytes=VMEM_LIMIT)


def vmem():
    return pl.BlockSpec(memory_space=pltpu.VMEM)


def smem():
    return pl.BlockSpec(memory_space=pltpu.SMEM)


def dot(a, b, dims=(((1,), (0,)), ((), ()))):
    return lax.dot_general(a, b, dims, preferred_element_type=F32)


def pack_two(left, right, out_ref):
    for h in range(HEADS):
        cut = slice(h * HEAD, (h + 1) * HEAD)
        out_ref[h] = jnp.concatenate([left[:, cut], right[:, cut]], axis=1)


def pack_kv_kernel(k_ref, v_ref, out_ref):
    pack_two(k_ref[0], v_ref[0], out_ref)


def pack_qd_kernel(q_ref, g_ref, w_ref, out_ref):
    grad_att = dot(g_ref[0], w_ref[...], NT).astype(BF16)
    pack_two(q_ref[0], grad_att, out_ref)


def attention_kernel(
    tiles_ref, place_ref, own_ref, prev_ref, next_ref, qd_ref,
    aq_ref, kv_own_ref, kv_prev_ref, kv_next_ref,
    packed, keys, turned, scores, weights, totals,
):
    quarter = own_ref.shape[0]
    per_quarter = quarter // TOK
    blocks = 3 * per_quarter
    first_query = place_ref[0] * quarter
    first_key = first_query - quarter

    lane = lax.broadcasted_iota(jnp.int32, (1, 128), 1)
    low = lane < HEAD

    def read_scenes(s, carry):
        start, starts, ends, lows, highs = carry
        end = start + tiles_ref[0, s] * TILE
        mine = lane == HEAD + s
        starts = jnp.where(mine, start, starts)
        ends = jnp.where(mine, end, ends)
        new_lows, new_highs = [], []
        for i in range(per_quarter):
            head = first_query + i * TOK
            tail = head + TOK - 1
            new_lows.append(jnp.where(jnp.logical_and(start <= head, head < end), start, lows[i]))
            new_highs.append(jnp.where(jnp.logical_and(start <= tail, tail < end), end, highs[i]))
        return end, starts, ends, tuple(new_lows), tuple(new_highs)

    zero = jnp.int32(0)
    nowhere = jnp.full((1, 128), 2**30, jnp.int32)
    _, starts, ends, lows, highs = lax.fori_loop(
        0, SCENES, read_scenes, (zero, nowhere, nowhere, (zero,) * per_quarter, (zero,) * per_quarter)
    )
    firsts = [(x - first_key) // TOK for x in lows]
    lasts = [(x - first_key + TOK - 1) // TOK for x in highs]

    scene_lane = jnp.logical_and(lane >= HEAD, lane < HEAD + SCENES)
    rows = lax.broadcasted_iota(jnp.int32, (TOK, 1), 0)

    def prepare(source_ref, base):
        def body(j, _):
            block = source_ref[pl.ds(pl.multiple_of((j - base) * TOK, TOK), TOK), :]
            position = first_key + j * TOK + rows
            inside = jnp.logical_and(position >= starts, position < ends)
            mark = jnp.where(inside, 1.0, 0.0).astype(BF16)
            packed[j] = block
            keys[j] = jnp.where(low, block, mark)
            turned[j] = block.T
            return 0
        return body

    begin, finish = firsts[0], lasts[-1]
    for part, source in enumerate((prev_ref, own_ref, next_ref)):
        base = part * per_quarter
        lax.fori_loop(
            jnp.maximum(begin, base), jnp.minimum(finish, base + per_quarter), prepare(source, base), 0
        )
    totals[...] = jnp.zeros_like(totals)

    for i in range(per_quarter):
        span = slice(i * TOK, (i + 1) * TOK)
        qd = qd_ref[span, :]
        position = first_query + i * TOK + rows
        same = jnp.logical_and(position >= starts, position < ends)
        other = jnp.where(jnp.logical_and(scene_lane, jnp.logical_not(same)), -BARRED, 0.0)
        query = jnp.where(low, qd.astype(F32) * HEAD**-0.5, other).astype(BF16)
        nil = jnp.zeros_like(qd)
        only_q = jnp.where(low, (qd.astype(F32) * HEAD**-0.5).astype(BF16), nil)
        only_d = jnp.where(low, nil, qd)
        pair = jnp.concatenate([only_q, only_d], axis=0)

        def first_pass(j, top):
            s = dot(keys[j], query, NT)
            scores[j] = s
            return jnp.maximum(top, jnp.max(s.reshape(TOK // 8, 8, TOK), axis=0))

        top = lax.fori_loop(firsts[i], lasts[i], first_pass, jnp.full((8, TOK), -1e30, F32))
        top = jnp.max(top, axis=0, keepdims=True)

        def second_pass(j, carry):
            total, attended = carry
            p = jnp.exp(scores[j] - top)
            total = total + jnp.sum(p.reshape(TOK // 8, 8, TOK), axis=0)
            p = p.astype(BF16)
            weights[j] = p
            attended = attended + dot(turned[j, HEAD:, :], p)
            return total, attended

        total, attended = lax.fori_loop(
            firsts[i], lasts[i], second_pass, (jnp.zeros((8, TOK), F32), jnp.zeros((HEAD, TOK), F32))
        )
        share = 1.0 / jnp.sum(total, axis=0, keepdims=True)
        attended = (attended * share).astype(BF16).astype(F32)
        grad_turned = qd.T[HEAD:, :].astype(F32)
        row_dot = jnp.sum(attended * grad_turned, axis=0, keepdims=True)

        def third_pass(j, grad_query):
            grad_probs = dot(packed[j], only_d, NT)
            probs = weights[j].astype(F32) * share
            grad_scores = (probs * (grad_probs - row_dot)).astype(BF16)
            both = jnp.concatenate([grad_scores, probs.astype(BF16)], axis=1)
            totals[j] += dot(both, pair)
            return grad_query + dot(turned[j, :HEAD, :], grad_scores)

        grad_query = lax.fori_loop(firsts[i], lasts[i], third_pass, jnp.zeros((HEAD, TOK), F32))
        out = jnp.concatenate([attended, grad_query * HEAD**-0.5], axis=0)
        aq_ref[span, :] = out.T.astype(BF16)

    for part, out_ref in enumerate((kv_prev_ref, kv_own_ref, kv_next_ref)):
        for j in range(per_quarter):
            out_ref[j] = totals[part * per_quarter + j].astype(BF16)


def attention(scene_tiles, place, own, prev, after, qd):
    quarter = own.shape[0]
    blocks = 3 * quarter // TOK
    grads = jax.ShapeDtypeStruct((quarter // TOK, TOK, 2 * HEAD), BF16)
    return pl.pallas_call(
        attention_kernel,
        out_shape=(jax.ShapeDtypeStruct(own.shape, BF16), grads, grads, grads),
        in_specs=[smem(), smem()] + [vmem()] * 4,
        out_specs=(vmem(),) * 4,
        scratch_shapes=[
            pltpu.VMEM((blocks, TOK, 2 * HEAD), BF16),
            pltpu.VMEM((blocks, TOK, 2 * HEAD), BF16),
            pltpu.VMEM((blocks, 2 * HEAD, TOK), BF16),
            pltpu.VMEM((blocks, TOK, TOK), F32),
            pltpu.VMEM((blocks, TOK, TOK), BF16),
            pltpu.VMEM((blocks, TOK, 2 * HEAD), F32),
        ],
        compiler_params=params(),
        name="attention",
    )(scene_tiles, place, own, prev, after, qd)


def finish_kernel(
    core_ref, aq_ref, kv_ref, normed_ref, gout_ref, wqkv_ref, gin_ref, keep_ref, send_ref, att, joint
):
    width = HEADS * HEAD
    for h in range(0, HEADS, 2):
        pair = slice(h * HEAD, (h + 2) * HEAD)
        one, two = aq_ref[h], aq_ref[h + 1]
        att[:, pair] = jnp.concatenate([one[:, :HEAD], two[:, :HEAD]], axis=1)
        joint[:, pair] = jnp.concatenate([one[:, HEAD:], two[:, HEAD:]], axis=1)
        one, two = kv_ref[h], kv_ref[h + 1]
        pair = slice(width + h * HEAD, width + (h + 2) * HEAD)
        joint[:, pair] = jnp.concatenate([one[:, :HEAD], two[:, :HEAD]], axis=1)
        pair = slice(2 * width + h * HEAD, 2 * width + (h + 2) * HEAD)
        joint[:, pair] = jnp.concatenate([one[:, HEAD:], two[:, HEAD:]], axis=1)
    core = core_ref[0]
    grads = joint[...]
    gin_ref[0] = dot(grads, wqkv_ref[...], NT).astype(BF16)
    half = width // 2
    for out_ref, which in ((keep_ref, core), (send_ref, 1 - core)):
        cut = pl.ds(pl.multiple_of(which * half, half), half)
        out_ref[:, : 3 * width] = dot(normed_ref[0, :, cut], grads, TN).astype(BF16)
        out_ref[:, 3 * width :] = dot(att[:, cut], gout_ref[0], TN).astype(BF16)


def finish(core, aq, kv, normed, gout, wqkv):
    width = HEADS * HEAD
    part = jax.ShapeDtypeStruct((width // 2, 4 * width), BF16)
    return pl.pallas_call(
        finish_kernel,
        out_shape=(jax.ShapeDtypeStruct(normed.shape, BF16), part, part),
        in_specs=[smem()] + [vmem()] * 5,
        out_specs=(vmem(),) * 3,
        scratch_shapes=[pltpu.VMEM((TOK, width), BF16), pltpu.VMEM((TOK, 3 * width), BF16)],
        compiler_params=params(),
        name="finish",
    )(core, aq, kv, normed, gout, wqkv)


def pack(kernel, *arrays):
    return pl.pallas_call(
        kernel,
        out_shape=jax.ShapeDtypeStruct((HEADS, TOK, 2 * HEAD), BF16),
        in_specs=[vmem()] * len(arrays),
        out_specs=vmem(),
        compiler_params=params(),
        name="pack",
    )(*arrays)


def spread(x, axes, count):
    return lax.all_to_all(jnp.broadcast_to(x[None], (count,) + x.shape), axes, 0, 0, tiled=True)


def shift(x, by):
    count = lax.axis_size("x")
    return lax.ppermute(x, "x", [(i, i + by) for i in range(count) if 0 <= i + by < count])


def local(normed, query_states, key_states, value_states, grad_output, w_qkv, w_out, scene_tiles):
    heads_axes, seq_axes = ("zl", "y"), ("x", "zl", "y")
    seq_count = lax.axis_size(seq_axes)
    quarter_shape = (lax.axis_size(heads_axes) * TOK, 2 * HEAD)
    place = lax.axis_index("x").reshape(1).astype(jnp.int32)
    core = lax.axis_index("c").reshape(1).astype(jnp.int32)

    def exchange(x):
        return lax.all_to_all(x, heads_axes, 0, 0, tiled=True)

    own = exchange(pack(pack_kv_kernel, key_states, value_states)).reshape(quarter_shape)
    prev, after = shift(own, 1), shift(own, -1)
    qd = exchange(pack(pack_qd_kernel, query_states, grad_output, w_out)).reshape(quarter_shape)
    aq, kv_own, kv_prev, kv_next = attention(scene_tiles, place, own, prev, after, qd)
    from_next, from_prev = shift(kv_prev, -1), shift(kv_next, 1)
    aq = exchange(aq.reshape(HEADS, TOK, 2 * HEAD))
    kv = (kv_own.astype(F32) + from_next.astype(F32) + from_prev.astype(F32)).astype(BF16)
    kv = exchange(kv)
    grad_in, keep, send = finish(core, aq, kv, normed, grad_output, w_qkv)

    swap = [(0, 1), (1, 0)]
    came = lax.ppermute(send, "c", swap)
    part = (keep.astype(F32) + came.astype(F32)).astype(BF16)
    rows, columns = part.shape
    part = part.reshape(seq_count, rows // seq_count, columns)
    part = jnp.sum(lax.all_to_all(part, seq_axes, 0, 0, tiled=True).astype(F32), axis=0)
    part = jnp.sum(spread(part.astype(BF16), ("zh",), lax.axis_size("zh")).astype(F32)
                   .reshape((-1,) + part.shape), axis=0)
    mine = spread(part.astype(BF16), seq_axes, seq_count).reshape(rows, columns)
    other = lax.ppermute(mine, "c", swap)
    first = core[0] == 0
    total = jnp.concatenate([jnp.where(first, mine, other), jnp.where(first, other, mine)], axis=0)
    total = total.astype(F32)
    joint_width = w_qkv.shape[1]
    return grad_in, total[:, :joint_width], total[:, joint_width:]


def solution(mesh):
    fine = Mesh(mesh.devices.reshape(4, 2, 4, 2, 4), ("zh", "c", "x", "zl", "y"))
    dp, seq = ("zh", "c"), ("x", "zl", "y")
    rows = P(dp, seq, None)
    in_specs = (rows,) * 5 + (P(), P(), P(dp, None))
    return jax.shard_map(local, mesh=fine, in_specs=in_specs, out_specs=(rows, P(), P()), check_vma=False)
```

```python
import jax
import jax.numpy as jnp
from jax import lax
from jax.experimental import pallas as pl
from jax.experimental.pallas import tpu as pltpu
from jax.sharding import Mesh
from jax.sharding import PartitionSpec as P

HEADS = 8
HEAD = 64
TILE = 32
TOK = 256
SCENES = 32
STEPS = (8, 4, 2, 1)
QUERIES = 512
BARRED = 16384.0
F32 = jnp.float32
BF16 = jnp.bfloat16
NT = (((1,), (1,)), ((), ()))
TN = (((0,), (0,)), ((), ()))
VMEM_LIMIT = 48 * 1024 * 1024


def params():
    return pltpu.CompilerParams(vmem_limit_bytes=VMEM_LIMIT)


def vmem():
    return pl.BlockSpec(memory_space=pltpu.VMEM)


def smem():
    return pl.BlockSpec(memory_space=pltpu.SMEM)


def anywhere():
    return pl.BlockSpec(memory_space=pl.ANY)


def dot(a, b, dims=(((1,), (0,)), ((), ()))):
    return lax.dot_general(a, b, dims, preferred_element_type=F32)


def pack_two(left, right, out_ref):
    for h in range(HEADS):
        cut = slice(h * HEAD, (h + 1) * HEAD)
        out_ref[h] = jnp.concatenate([left[:, cut], right[:, cut]], axis=1)


def pack_kv_kernel(k_ref, v_ref, out_ref):
    pack_two(k_ref[0], v_ref[0], out_ref)


def pack_qd_kernel(q_ref, g_ref, w_ref, out_ref):
    grad_att = dot(g_ref[0], w_ref[...], NT).astype(BF16)
    pack_two(q_ref[0], grad_att, out_ref)


def attention_kernel(
    tiles_ref, place_ref, own_hbm, prev_hbm, next_hbm, qd_hbm,
    aq_hbm, kv_own_hbm, kv_prev_hbm, kv_next_hbm,
    own_ref, prev_ref, next_ref, qd_ref, aq_ref, kv_ref, came, left,
    packed, keys, turned, scores, weights, totals,
):
    arrivals = [
        pltpu.make_async_copy(source, target, came.at[n])
        for n, (source, target) in enumerate(
            ((own_hbm, own_ref), (qd_hbm, qd_ref), (prev_hbm, prev_ref), (next_hbm, next_ref))
        )
    ]
    for copy in arrivals:
        copy.start()
    quarter = own_ref.shape[0]
    per_quarter = quarter // TOK
    query_blocks = quarter // QUERIES
    first_query = place_ref[0] * quarter
    first_key = first_query - quarter

    lane = lax.broadcasted_iota(jnp.int32, (1, 128), 1)
    low = lane < HEAD

    def read_scenes(s, carry):
        start, starts, ends, lows, highs = carry
        end = start + tiles_ref[0, s] * TILE
        mine = lane == HEAD + s
        starts = jnp.where(mine, start, starts)
        ends = jnp.where(mine, end, ends)
        new_lows, new_highs = [], []
        for i in range(query_blocks):
            head = first_query + i * QUERIES
            tail = head + QUERIES - 1
            new_lows.append(jnp.where(jnp.logical_and(start <= head, head < end), start, lows[i]))
            new_highs.append(jnp.where(jnp.logical_and(start <= tail, tail < end), end, highs[i]))
        return end, starts, ends, tuple(new_lows), tuple(new_highs)

    zero = jnp.int32(0)
    nowhere = jnp.full((1, 128), 2**30, jnp.int32)
    _, starts, ends, lows, highs = lax.fori_loop(
        0, SCENES, read_scenes, (zero, nowhere, nowhere, (zero,) * query_blocks, (zero,) * query_blocks)
    )
    firsts = [(x - first_key) // TOK for x in lows]
    lasts = [(x - first_key + TOK - 1) // TOK for x in highs]

    scene_lane = jnp.logical_and(lane >= HEAD, lane < HEAD + SCENES)
    rows = lax.broadcasted_iota(jnp.int32, (TOK, 1), 0)

    query_rows = lax.broadcasted_iota(jnp.int32, (QUERIES, 1), 0)

    def prepare(source_ref, base):
        def body(j, _):
            block = source_ref[pl.ds(pl.multiple_of((j - base) * TOK, TOK), TOK), :]
            position = first_key + j * TOK + rows
            inside = jnp.logical_and(position >= starts, position < ends)
            mark = jnp.where(inside, 1.0, 0.0).astype(BF16)
            packed[j] = block
            keys[j] = jnp.where(low, block, mark)
            turned[j] = block.T
            return 0
        return body

    totals[...] = jnp.zeros_like(totals)
    for copy in arrivals:
        copy.wait()
    begin, finish = firsts[0], lasts[-1]
    for part, source in enumerate((prev_ref, own_ref, next_ref)):
        base = part * per_quarter
        lax.fori_loop(
            jnp.maximum(begin, base), jnp.minimum(finish, base + per_quarter), prepare(source, base), 0
        )

    def sweep(first, last, body, carry):
        for step in STEPS:
            groups = (last - first) // step

            def many(t, c, first=first, step=step):
                for u in range(step):
                    c = body(first + t * step + u, c)
                return c

            carry = lax.fori_loop(0, groups, many, carry)
            first = first + groups * step
        return carry

    leaving = []
    for i in range(query_blocks):
        span = slice(i * QUERIES, (i + 1) * QUERIES)
        qd = qd_ref[span, :]
        position = first_query + i * QUERIES + query_rows
        same = jnp.logical_and(position >= starts, position < ends)
        other = jnp.where(jnp.logical_and(scene_lane, jnp.logical_not(same)), -BARRED, 0.0)
        scaled = qd.astype(F32) * HEAD**-0.5
        query = jnp.where(low, scaled, other).T.astype(BF16)
        nil = jnp.zeros_like(qd)
        only_q = jnp.where(low, scaled.astype(BF16), nil)
        only_d = jnp.where(low, nil, qd)
        pair = jnp.concatenate([only_q, only_d], axis=0)
        grad = only_d.T

        def first_pass(j, top):
            s = dot(keys[j], query)
            scores[j] = s
            return jnp.maximum(top, jnp.max(s.reshape(TOK // 8, 8, QUERIES), axis=0))

        top = sweep(firsts[i], lasts[i], first_pass, jnp.full((8, QUERIES), -1e30, F32))
        top = jnp.max(top, axis=0, keepdims=True)

        def second_pass(j, carry):
            total, attended = carry
            p = jnp.exp(scores[j] - top)
            total = total + jnp.sum(p.reshape(TOK // 8, 8, QUERIES), axis=0)
            p = p.astype(BF16)
            weights[j] = p
            attended = attended + dot(turned[j, HEAD:, :], p)
            return total, attended

        total, attended = sweep(
            firsts[i], lasts[i], second_pass, (jnp.zeros((8, QUERIES), F32), jnp.zeros((HEAD, QUERIES), F32))
        )
        share = 1.0 / jnp.sum(total, axis=0, keepdims=True)
        attended = (attended * share).astype(BF16).astype(F32)
        row_dot = jnp.sum(attended * grad[HEAD:, :].astype(F32), axis=0, keepdims=True)

        def third_pass(j, grad_query):
            grad_probs = dot(packed[j], grad)
            probs = weights[j].astype(F32) * share
            grad_scores = (probs * (grad_probs - row_dot)).astype(BF16)
            both = jnp.concatenate([grad_scores, probs.astype(BF16)], axis=1)
            totals[j] += dot(both, pair)
            return grad_query + dot(turned[j, :HEAD, :], grad_scores)

        grad_query = sweep(firsts[i], lasts[i], third_pass, jnp.zeros((HEAD, QUERIES), F32))
        out = jnp.concatenate([attended, grad_query * HEAD**-0.5], axis=0)
        aq_ref[span, :] = out.T.astype(BF16)
        leaving.append(pltpu.make_async_copy(aq_ref.at[span], aq_hbm.at[span], left.at[i]))
        leaving[-1].start()

    for part, out_hbm in enumerate((kv_prev_hbm, kv_own_hbm, kv_next_hbm)):
        for j in range(per_quarter):
            kv_ref[part, j] = totals[part * per_quarter + j].astype(BF16)
        leaving.append(pltpu.make_async_copy(kv_ref.at[part], out_hbm, left.at[query_blocks + part]))
        leaving[-1].start()
    for copy in leaving:
        copy.wait()


def attention(scene_tiles, place, own, prev, after, qd):
    quarter = own.shape[0]
    blocks = 3 * quarter // TOK
    grads = jax.ShapeDtypeStruct((quarter // TOK, TOK, 2 * HEAD), BF16)
    return pl.pallas_call(
        attention_kernel,
        out_shape=(jax.ShapeDtypeStruct(own.shape, BF16), grads, grads, grads),
        in_specs=[smem(), smem()] + [anywhere()] * 4,
        out_specs=(anywhere(),) * 4,
        scratch_shapes=[pltpu.VMEM(own.shape, BF16)] * 5 + [
            pltpu.VMEM((3, quarter // TOK, TOK, 2 * HEAD), BF16),
            pltpu.SemaphoreType.DMA((4,)),
            pltpu.SemaphoreType.DMA((quarter // QUERIES + 3,)),
            pltpu.VMEM((blocks, TOK, 2 * HEAD), BF16),
            pltpu.VMEM((blocks, TOK, 2 * HEAD), BF16),
            pltpu.VMEM((blocks, 2 * HEAD, TOK), BF16),
            pltpu.VMEM((blocks, TOK, QUERIES), F32),
            pltpu.VMEM((blocks, TOK, QUERIES), BF16),
            pltpu.VMEM((blocks, TOK, 2 * HEAD), F32),
        ],
        compiler_params=params(),
        name="attention",
    )(scene_tiles, place, own, prev, after, qd)


def finish_kernel(
    core_ref, aq_ref, kv_ref, normed_ref, gout_ref, wqkv_ref, gin_ref, keep_ref, send_ref, att, joint
):
    width = HEADS * HEAD
    for h in range(0, HEADS, 2):
        pair = slice(h * HEAD, (h + 2) * HEAD)
        one, two = aq_ref[h], aq_ref[h + 1]
        att[:, pair] = jnp.concatenate([one[:, :HEAD], two[:, :HEAD]], axis=1)
        joint[:, pair] = jnp.concatenate([one[:, HEAD:], two[:, HEAD:]], axis=1)
        one, two = kv_ref[h], kv_ref[h + 1]
        pair = slice(width + h * HEAD, width + (h + 2) * HEAD)
        joint[:, pair] = jnp.concatenate([one[:, :HEAD], two[:, :HEAD]], axis=1)
        pair = slice(2 * width + h * HEAD, 2 * width + (h + 2) * HEAD)
        joint[:, pair] = jnp.concatenate([one[:, HEAD:], two[:, HEAD:]], axis=1)
    core = core_ref[0]
    grads = joint[...]
    gin_ref[0] = dot(grads, wqkv_ref[...], NT).astype(BF16)
    half = width // 2
    for out_ref, which in ((keep_ref, core), (send_ref, 1 - core)):
        cut = pl.ds(pl.multiple_of(which * half, half), half)
        out_ref[:, : 3 * width] = dot(normed_ref[0, :, cut], grads, TN).astype(BF16)
        out_ref[:, 3 * width :] = dot(att[:, cut], gout_ref[0], TN).astype(BF16)


def finish(core, aq, kv, normed, gout, wqkv):
    width = HEADS * HEAD
    part = jax.ShapeDtypeStruct((width // 2, 4 * width), BF16)
    return pl.pallas_call(
        finish_kernel,
        out_shape=(jax.ShapeDtypeStruct(normed.shape, BF16), part, part),
        in_specs=[smem()] + [vmem()] * 5,
        out_specs=(vmem(),) * 3,
        scratch_shapes=[pltpu.VMEM((TOK, width), BF16), pltpu.VMEM((TOK, 3 * width), BF16)],
        compiler_params=params(),
        name="finish",
    )(core, aq, kv, normed, gout, wqkv)


def pack(kernel, *arrays):
    return pl.pallas_call(
        kernel,
        out_shape=jax.ShapeDtypeStruct((HEADS, TOK, 2 * HEAD), BF16),
        in_specs=[vmem()] * len(arrays),
        out_specs=vmem(),
        compiler_params=params(),
        name="pack",
    )(*arrays)


def spread(x, axes, count):
    return lax.all_to_all(jnp.broadcast_to(x[None], (count,) + x.shape), axes, 0, 0, tiled=True)


def shift(x, by):
    count = lax.axis_size("x")
    return lax.ppermute(x, "x", [(i, i + by) for i in range(count) if 0 <= i + by < count])


def local(normed, query_states, key_states, value_states, grad_output, w_qkv, w_out, scene_tiles):
    heads_axes, seq_axes = ("zl", "y"), ("x", "zl", "y")
    seq_count = lax.axis_size(seq_axes)
    quarter_shape = (lax.axis_size(heads_axes) * TOK, 2 * HEAD)
    place = lax.axis_index("x").reshape(1).astype(jnp.int32)
    core = lax.axis_index("c").reshape(1).astype(jnp.int32)

    def exchange(x):
        return lax.all_to_all(x, heads_axes, 0, 0, tiled=True)

    own = exchange(pack(pack_kv_kernel, key_states, value_states)).reshape(quarter_shape)
    prev, after = shift(own, 1), shift(own, -1)
    qd = exchange(pack(pack_qd_kernel, query_states, grad_output, w_out)).reshape(quarter_shape)
    aq, kv_own, kv_prev, kv_next = attention(scene_tiles, place, own, prev, after, qd)
    from_next, from_prev = shift(kv_prev, -1), shift(kv_next, 1)
    aq = exchange(aq.reshape(HEADS, TOK, 2 * HEAD))
    kv = (kv_own.astype(F32) + from_next.astype(F32) + from_prev.astype(F32)).astype(BF16)
    kv = exchange(kv)
    grad_in, keep, send = finish(core, aq, kv, normed, grad_output, w_qkv)

    swap = [(0, 1), (1, 0)]
    came = lax.ppermute(send, "c", swap)
    part = (keep.astype(F32) + came.astype(F32)).astype(BF16)
    rows, columns = part.shape
    part = part.reshape(seq_count, rows // seq_count, columns)
    part = jnp.sum(lax.all_to_all(part, seq_axes, 0, 0, tiled=True).astype(F32), axis=0)
    part = part.astype(BF16)
    for step in (1, 2):
        partner = [(i, i ^ step) for i in range(lax.axis_size("zh"))]
        part = (part.astype(F32) + lax.ppermute(part, "zh", partner).astype(F32)).astype(BF16)
    mine = spread(part, seq_axes, seq_count).reshape(rows, columns)
    other = lax.ppermute(mine, "c", swap)
    first = core[0] == 0
    total = jnp.concatenate([jnp.where(first, mine, other), jnp.where(first, other, mine)], axis=0)
    total = total.astype(F32)
    joint_width = w_qkv.shape[1]
    return grad_in, total[:, :joint_width], total[:, joint_width:]


def solution(mesh):
    fine = Mesh(mesh.devices.reshape(4, 2, 4, 2, 4), ("zh", "c", "x", "zl", "y"))
    dp, seq = ("zh", "c"), ("x", "zl", "y")
    rows = P(dp, seq, None)
    in_specs = (rows,) * 5 + (P(), P(), P(dp, None))
    return jax.shard_map(local, mesh=fine, in_specs=in_specs, out_specs=(rows, P(), P()), check_vma=False)
```

```python
import jax
import jax.numpy as jnp
from jax import lax
from jax.experimental import pallas as pl
from jax.experimental.pallas import tpu as pltpu
from jax.sharding import Mesh
from jax.sharding import PartitionSpec as P

HEADS = 8
HEAD = 64
TILE = 32
TOK = 256
SCENES = 32
STEPS = (8, 4, 2, 1)
QUERIES = 512
BARRED = 16384.0
F32 = jnp.float32
BF16 = jnp.bfloat16
NT = (((1,), (1,)), ((), ()))
TN = (((0,), (0,)), ((), ()))
VMEM_LIMIT = 48 * 1024 * 1024


def params():
    return pltpu.CompilerParams(vmem_limit_bytes=VMEM_LIMIT)


def vmem():
    return pl.BlockSpec(memory_space=pltpu.VMEM)


def smem():
    return pl.BlockSpec(memory_space=pltpu.SMEM)


def anywhere():
    return pl.BlockSpec(memory_space=pltpu.HBM)


def dot(a, b, dims=(((1,), (0,)), ((), ()))):
    return lax.dot_general(a, b, dims, preferred_element_type=F32)


def pack_two(left, right, out_ref):
    for h in range(HEADS):
        cut = slice(h * HEAD, (h + 1) * HEAD)
        out_ref[h] = jnp.concatenate([left[:, cut], right[:, cut]], axis=1)


def pack_kv_kernel(k_ref, v_ref, out_ref):
    pack_two(k_ref[0], v_ref[0], out_ref)


def pack_qd_kernel(q_ref, g_ref, w_ref, out_ref):
    grad_att = dot(g_ref[0], w_ref[...], NT).astype(BF16)
    pack_two(q_ref[0], grad_att, out_ref)


def attention_kernel(
    tiles_ref, place_ref, own_hbm, prev_hbm, next_hbm, qd_hbm,
    aq_hbm, kv_own_hbm, kv_prev_hbm, kv_next_hbm,
    own_ref, prev_ref, next_ref, qd_ref, aq_ref, kv_ref, came, left,
    packed, keys, turned, scores, weights, totals,
):
    arrivals = [
        pltpu.make_async_copy(source, target, came.at[n])
        for n, (source, target) in enumerate(
            ((own_hbm, own_ref), (qd_hbm, qd_ref), (prev_hbm, prev_ref), (next_hbm, next_ref))
        )
    ]
    for copy in arrivals:
        copy.start()
    quarter = own_ref.shape[0]
    per_quarter = quarter // TOK
    query_blocks = quarter // QUERIES
    first_query = place_ref[0] * quarter
    first_key = first_query - quarter

    lane = lax.broadcasted_iota(jnp.int32, (1, 128), 1)
    low = lane < HEAD

    def read_scenes(s, carry):
        start, starts, ends, lows, highs = carry
        end = start + tiles_ref[0, s] * TILE
        mine = lane == HEAD + s
        starts = jnp.where(mine, start, starts)
        ends = jnp.where(mine, end, ends)
        new_lows, new_highs = [], []
        for i in range(query_blocks):
            head = first_query + i * QUERIES
            tail = head + QUERIES - 1
            new_lows.append(jnp.where(jnp.logical_and(start <= head, head < end), start, lows[i]))
            new_highs.append(jnp.where(jnp.logical_and(start <= tail, tail < end), end, highs[i]))
        return end, starts, ends, tuple(new_lows), tuple(new_highs)

    zero = jnp.int32(0)
    nowhere = jnp.full((1, 128), 2**30, jnp.int32)
    _, starts, ends, lows, highs = lax.fori_loop(
        0, SCENES, read_scenes, (zero, nowhere, nowhere, (zero,) * query_blocks, (zero,) * query_blocks)
    )
    firsts = [(x - first_key) // TOK for x in lows]
    lasts = [(x - first_key + TOK - 1) // TOK for x in highs]

    scene_lane = jnp.logical_and(lane >= HEAD, lane < HEAD + SCENES)
    rows = lax.broadcasted_iota(jnp.int32, (TOK, 1), 0)

    query_rows = lax.broadcasted_iota(jnp.int32, (QUERIES, 1), 0)

    def prepare(source_ref, base):
        def body(j, _):
            block = source_ref[pl.ds(pl.multiple_of((j - base) * TOK, TOK), TOK), :]
            position = first_key + j * TOK + rows
            inside = jnp.logical_and(position >= starts, position < ends)
            mark = jnp.where(inside, 1.0, 0.0).astype(BF16)
            packed[j] = block
            keys[j] = jnp.where(low, block, mark)
            turned[j] = block.T
            return 0
        return body

    totals[...] = jnp.zeros_like(totals)
    for copy in arrivals:
        copy.wait()
    begin, finish = firsts[0], lasts[-1]
    for part, source in enumerate((prev_ref, own_ref, next_ref)):
        base = part * per_quarter
        lax.fori_loop(
            jnp.maximum(begin, base), jnp.minimum(finish, base + per_quarter), prepare(source, base), 0
        )

    def sweep(first, last, body, carry):
        for step in STEPS:
            groups = (last - first) // step

            def many(t, c, first=first, step=step):
                for u in range(step):
                    c = body(first + t * step + u, c)
                return c

            carry = lax.fori_loop(0, groups, many, carry)
            first = first + groups * step
        return carry

    leaving = []
    for i in range(query_blocks):
        span = slice(i * QUERIES, (i + 1) * QUERIES)
        qd = qd_ref[span, :]
        position = first_query + i * QUERIES + query_rows
        same = jnp.logical_and(position >= starts, position < ends)
        other = jnp.where(jnp.logical_and(scene_lane, jnp.logical_not(same)), -BARRED, 0.0)
        scaled = qd.astype(F32) * HEAD**-0.5
        query = jnp.where(low, scaled, other).T.astype(BF16)
        nil = jnp.zeros_like(qd)
        only_q = jnp.where(low, scaled.astype(BF16), nil)
        only_d = jnp.where(low, nil, qd)
        pair = jnp.concatenate([only_q, only_d], axis=0)
        grad = only_d.T

        def first_pass(j, top):
            s = dot(keys[j], query)
            scores[j] = s
            return jnp.maximum(top, jnp.max(s.reshape(TOK // 8, 8, QUERIES), axis=0))

        top = sweep(firsts[i], lasts[i], first_pass, jnp.full((8, QUERIES), -1e30, F32))
        top = jnp.max(top, axis=0, keepdims=True)

        def second_pass(j, carry):
            total, attended = carry
            p = jnp.exp(scores[j] - top)
            total = total + jnp.sum(p.reshape(TOK // 8, 8, QUERIES), axis=0)
            p = p.astype(BF16)
            weights[j] = p
            attended = attended + dot(turned[j, HEAD:, :], p)
            return total, attended

        total, attended = sweep(
            firsts[i], lasts[i], second_pass, (jnp.zeros((8, QUERIES), F32), jnp.zeros((HEAD, QUERIES), F32))
        )
        share = 1.0 / jnp.sum(total, axis=0, keepdims=True)
        attended = (attended * share).astype(BF16).astype(F32)
        row_dot = jnp.sum(attended * grad[HEAD:, :].astype(F32), axis=0, keepdims=True)

        def third_pass(j, grad_query):
            grad_probs = dot(packed[j], grad)
            probs = weights[j].astype(F32) * share
            grad_scores = (probs * (grad_probs - row_dot)).astype(BF16)
            both = jnp.concatenate([grad_scores, probs.astype(BF16)], axis=1)
            totals[j] += dot(both, pair)
            return grad_query + dot(turned[j, :HEAD, :], grad_scores)

        grad_query = sweep(firsts[i], lasts[i], third_pass, jnp.zeros((HEAD, QUERIES), F32))
        out = jnp.concatenate([attended, grad_query * HEAD**-0.5], axis=0)
        aq_ref[span, :] = out.T.astype(BF16)
        leaving.append(pltpu.make_async_copy(aq_ref.at[span], aq_hbm.at[span], left.at[i]))
        leaving[-1].start()

    for part, out_hbm in enumerate((kv_prev_hbm, kv_own_hbm, kv_next_hbm)):
        for j in range(per_quarter):
            kv_ref[part, j] = totals[part * per_quarter + j].astype(BF16)
        leaving.append(pltpu.make_async_copy(kv_ref.at[part], out_hbm, left.at[query_blocks + part]))
        leaving[-1].start()
    for copy in leaving:
        copy.wait()


def attention(scene_tiles, place, own, prev, after, qd):
    quarter = own.shape[0]
    blocks = 3 * quarter // TOK
    grads = jax.ShapeDtypeStruct((quarter // TOK, TOK, 2 * HEAD), BF16)
    return pl.pallas_call(
        attention_kernel,
        out_shape=(jax.ShapeDtypeStruct(own.shape, BF16), grads, grads, grads),
        in_specs=[smem(), smem()] + [anywhere()] * 4,
        out_specs=(anywhere(),) * 4,
        scratch_shapes=[pltpu.VMEM(own.shape, BF16)] * 5 + [
            pltpu.VMEM((3, quarter // TOK, TOK, 2 * HEAD), BF16),
            pltpu.SemaphoreType.DMA((4,)),
            pltpu.SemaphoreType.DMA((quarter // QUERIES + 3,)),
            pltpu.VMEM((blocks, TOK, 2 * HEAD), BF16),
            pltpu.VMEM((blocks, TOK, 2 * HEAD), BF16),
            pltpu.VMEM((blocks, 2 * HEAD, TOK), BF16),
            pltpu.VMEM((blocks, TOK, QUERIES), F32),
            pltpu.VMEM((blocks, TOK, QUERIES), BF16),
            pltpu.VMEM((blocks, TOK, 2 * HEAD), F32),
        ],
        compiler_params=params(),
        cost_estimate=pl.CostEstimate(
            flops=6 * 2 * quarter * 3 * quarter * 2 * HEAD,
            transcendentals=3 * quarter * quarter,
            bytes_accessed=8 * own.size * 2,
        ),
        name="attention",
    )(scene_tiles, place, own, prev, after, qd)


def weight_kernel(
    core_ref, aq_ref, own_ref, next_ref, prev_ref, factors_ref, kv_ref, keep_ref, send_ref, whole
):
    shape = aq_ref.shape
    kv = (own_ref[...].astype(F32) + next_ref[...].astype(F32) + prev_ref[...].astype(F32)).astype(BF16)
    kv_ref[...] = kv
    aq = aq_ref[...]
    width = HEADS * HEAD
    normed = factors_ref[:, :, :width].reshape(shape[0], width)
    gout = factors_ref[:, :, width:].reshape(shape[0], width)
    whole[0, :HEAD] = dot(aq[:, :HEAD], gout, TN).astype(BF16)
    whole[0, HEAD:] = dot(aq[:, HEAD:], normed, TN).astype(BF16)
    whole[1] = dot(kv.reshape(shape), normed, TN).astype(BF16)
    keep_ref[...] = whole[core_ref[0]]
    send_ref[...] = whole[1 - core_ref[0]]


def weight_sums(core, aq, own, from_next, from_prev, factors):
    part = jax.ShapeDtypeStruct((2 * HEAD, HEADS * HEAD), BF16)
    return pl.pallas_call(
        weight_kernel,
        out_shape=(jax.ShapeDtypeStruct(own.shape, BF16), part, part),
        in_specs=[smem()] + [vmem()] * 5,
        out_specs=(vmem(),) * 3,
        scratch_shapes=[pltpu.VMEM((2,) + part.shape, BF16)],
        compiler_params=params(),
        name="weight_sums",
    )(core, aq, own, from_next, from_prev, factors)


def input_kernel(aq_ref, kv_ref, wqkv_ref, gin_ref, joint):
    width = HEADS * HEAD
    for h in range(0, HEADS, 2):
        for part, ref, cut in ((0, aq_ref, 1), (1, kv_ref, 0), (2, kv_ref, 1)):
            cut = slice(cut * HEAD, (cut + 1) * HEAD)
            spot = slice(part * width + h * HEAD, part * width + (h + 2) * HEAD)
            joint[:, spot] = jnp.concatenate([ref[h, :, cut], ref[h + 1, :, cut]], axis=1)
    gin_ref[0] = dot(joint[...], wqkv_ref[...], NT).astype(BF16)


def input_grad(aq, kv, wqkv):
    width = HEADS * HEAD
    return pl.pallas_call(
        input_kernel,
        out_shape=jax.ShapeDtypeStruct((1, TOK, width), BF16),
        in_specs=[vmem()] * 3,
        out_specs=vmem(),
        scratch_shapes=[pltpu.VMEM((TOK, 3 * width), BF16)],
        compiler_params=params(),
        name="input_grad",
    )(aq, kv, wqkv)


def place_kernel(core_ref, mine_ref, other_ref, qkv_ref, out_ref):
    width = HEADS * HEAD

    def lay(first, second):
        def head_rows(ref, h, cut):
            return [ref[2 * cut, h], ref[2 * cut + 1, h]]

        for h in range(HEADS):
            out_ref[h * HEAD : (h + 1) * HEAD, :] = jnp.concatenate(head_rows(first, h, 0)).astype(F32)
        for h in range(0, HEADS, 2):
            for part, ref, cut in ((0, first, 1), (1, second, 0), (2, second, 1)):
                both = jnp.concatenate(head_rows(ref, h, cut) + head_rows(ref, h + 1, cut))
                spot = slice(part * width + h * HEAD, part * width + (h + 2) * HEAD)
                qkv_ref[:, spot] = both.T.astype(F32)

    pl.when(core_ref[0] == 0)(lambda: lay(mine_ref, other_ref))
    pl.when(core_ref[0] != 0)(lambda: lay(other_ref, mine_ref))


def place_sums(core, mine, other):
    width = HEADS * HEAD
    return pl.pallas_call(
        place_kernel,
        out_shape=(
            jax.ShapeDtypeStruct((width, 3 * width), F32),
            jax.ShapeDtypeStruct((width, width), F32),
        ),
        in_specs=[smem()] + [vmem()] * 2,
        out_specs=(vmem(),) * 2,
        compiler_params=params(),
        name="place_sums",
    )(core, mine, other)


def pack(kernel, *arrays):
    return pl.pallas_call(
        kernel,
        out_shape=jax.ShapeDtypeStruct((HEADS, TOK, 2 * HEAD), BF16),
        in_specs=[vmem()] * len(arrays),
        out_specs=vmem(),
        compiler_params=params(),
        name="pack",
    )(*arrays)


def spread(x, axes, count):
    return lax.all_to_all(jnp.broadcast_to(x[None], (count,) + x.shape), axes, 0, 0, tiled=True)


def shift(x, by):
    count = lax.axis_size("x")
    return lax.ppermute(x, "x", [(i, i + by) for i in range(count) if 0 <= i + by < count])


def local(normed, query_states, key_states, value_states, grad_output, w_qkv, w_out, scene_tiles):
    heads_axes, seq_axes = ("zl", "y"), ("x", "zl", "y")
    seq_count = lax.axis_size(seq_axes)
    quarter_shape = (lax.axis_size(heads_axes) * TOK, 2 * HEAD)
    place = lax.axis_index("x").reshape(1).astype(jnp.int32)
    core = lax.axis_index("c").reshape(1).astype(jnp.int32)

    def exchange(x):
        return lax.all_to_all(x, heads_axes, 0, 0, tiled=True)

    own = exchange(pack(pack_kv_kernel, key_states, value_states)).reshape(quarter_shape)
    qd = pack(pack_qd_kernel, query_states, grad_output, w_out)
    own, qd = lax.optimization_barrier((own, qd))
    prev, after = shift(own, 1), shift(own, -1)
    qd = exchange(qd).reshape(quarter_shape)
    factors = jnp.concatenate([normed[0], grad_output[0]], axis=1)
    factors = jnp.broadcast_to(factors[None], (HEADS,) + factors.shape)
    qd, prev, after, factors = lax.optimization_barrier((qd, prev, after, factors))
    factors = exchange(factors)
    aq, kv_own, kv_prev, kv_next = attention(scene_tiles, place, own, prev, after, qd)
    aq, factors = lax.optimization_barrier((aq, factors))
    from_next, from_prev = shift(kv_prev, -1), shift(kv_next, 1)
    aq_home = exchange(aq.reshape(HEADS, TOK, 2 * HEAD))
    aq_home, from_next, from_prev = lax.optimization_barrier((aq_home, from_next, from_prev))
    kv, keep, send = weight_sums(core, aq, kv_own, from_next, from_prev, factors)
    kv_home = exchange(kv)

    swap = [(0, 1), (1, 0)]
    came = lax.ppermute(send, "c", swap)
    part = (keep.astype(F32) + came.astype(F32)).astype(BF16)
    rows, columns = part.shape
    quarters = lax.axis_size("x")
    part = part.reshape(quarters, rows // quarters, columns)
    part = jnp.sum(lax.all_to_all(part, ("x",), 0, 0, tiled=True).astype(F32), axis=0).astype(BF16)
    for step in (1, 2):
        partner = [(i, i ^ step) for i in range(lax.axis_size("zh"))]
        part = (part.astype(F32) + lax.ppermute(part, "zh", partner).astype(F32)).astype(BF16)
    part, kv_home = lax.optimization_barrier((part, kv_home))
    grad_in = input_grad(aq_home, kv_home, w_qkv)
    mine = spread(part, seq_axes, seq_count).reshape((quarters, HEADS) + part.shape)
    other = lax.ppermute(mine, "c", swap)
    total_qkv, total_out = place_sums(core, mine, other)
    return grad_in, total_qkv, total_out


def solution(mesh):
    fine = Mesh(mesh.devices.reshape(4, 2, 4, 2, 4), ("zh", "c", "x", "zl", "y"))
    dp, seq = ("zh", "c"), ("x", "zl", "y")
    rows = P(dp, seq, None)
    in_specs = (rows,) * 5 + (P(), P(), P(dp, None))
    return jax.shard_map(local, mesh=fine, in_specs=in_specs, out_specs=(rows, P(), P()), check_vma=False)
```

```python
import jax
import jax.numpy as jnp
from jax import lax
from jax.experimental import pallas as pl
from jax.experimental.pallas import tpu as pltpu
from jax.sharding import Mesh
from jax.sharding import PartitionSpec as P

HEADS = 8
HEAD = 64
TILE = 32
TOK = 256
SCENES = 32
STEPS = (8, 4, 2, 1)
QUERIES = 512
BARRED = 16384.0
F32 = jnp.float32
BF16 = jnp.bfloat16
NT = (((1,), (1,)), ((), ()))
TN = (((0,), (0,)), ((), ()))
VMEM_LIMIT = 48 * 1024 * 1024


def params():
    return pltpu.CompilerParams(vmem_limit_bytes=VMEM_LIMIT)


def vmem():
    return pl.BlockSpec(memory_space=pltpu.VMEM)


def smem():
    return pl.BlockSpec(memory_space=pltpu.SMEM)


def anywhere():
    return pl.BlockSpec(memory_space=pltpu.HBM)


def dot(a, b, dims=(((1,), (0,)), ((), ()))):
    return lax.dot_general(a, b, dims, preferred_element_type=F32)


def pack_two(left, right, out_ref):
    for h in range(HEADS):
        cut = slice(h * HEAD, (h + 1) * HEAD)
        out_ref[h] = jnp.concatenate([left[:, cut], right[:, cut]], axis=1)


def pack_kv_kernel(k_ref, v_ref, out_ref):
    pack_two(k_ref[0], v_ref[0], out_ref)


def pack_qd_kernel(q_ref, g_ref, w_ref, out_ref):
    grad_att = dot(g_ref[0], w_ref[...], NT).astype(BF16)
    pack_two(q_ref[0], grad_att, out_ref)


def attention_kernel(
    tiles_ref, place_ref, own_hbm, prev_hbm, next_hbm, qd_hbm,
    aq_hbm, kv_own_hbm, kv_prev_hbm, kv_next_hbm,
    own_ref, prev_ref, next_ref, qd_ref, aq_ref, kv_ref, came, left,
    packed, keys, turned, scores, weights, totals,
):
    arrivals = [
        pltpu.make_async_copy(source, target, came.at[n])
        for n, (source, target) in enumerate(
            ((own_hbm, own_ref), (qd_hbm, qd_ref), (prev_hbm, prev_ref), (next_hbm, next_ref))
        )
    ]
    for copy in arrivals:
        copy.start()
    quarter = own_ref.shape[0]
    per_quarter = quarter // TOK
    query_blocks = quarter // QUERIES
    first_query = place_ref[0] * quarter
    first_key = first_query - quarter

    lane = lax.broadcasted_iota(jnp.int32, (1, 128), 1)
    low = lane < HEAD

    def read_scenes(s, carry):
        start, starts, ends, lows, highs = carry
        end = start + tiles_ref[0, s] * TILE
        mine = lane == HEAD + s
        starts = jnp.where(mine, start, starts)
        ends = jnp.where(mine, end, ends)
        new_lows, new_highs = [], []
        for i in range(query_blocks):
            head = first_query + i * QUERIES
            tail = head + QUERIES - 1
            new_lows.append(jnp.where(jnp.logical_and(start <= head, head < end), start, lows[i]))
            new_highs.append(jnp.where(jnp.logical_and(start <= tail, tail < end), end, highs[i]))
        return end, starts, ends, tuple(new_lows), tuple(new_highs)

    zero = jnp.int32(0)
    nowhere = jnp.full((1, 128), 2**30, jnp.int32)
    _, starts, ends, lows, highs = lax.fori_loop(
        0, SCENES, read_scenes, (zero, nowhere, nowhere, (zero,) * query_blocks, (zero,) * query_blocks)
    )
    firsts = [(x - first_key) // TOK for x in lows]
    lasts = [(x - first_key + TOK - 1) // TOK for x in highs]

    scene_lane = jnp.logical_and(lane >= HEAD, lane < HEAD + SCENES)
    rows = lax.broadcasted_iota(jnp.int32, (TOK, 1), 0)

    query_rows = lax.broadcasted_iota(jnp.int32, (QUERIES, 1), 0)

    def prepare(source_ref, base):
        def body(j, _):
            block = source_ref[pl.ds(pl.multiple_of((j - base) * TOK, TOK), TOK), :]
            position = first_key + j * TOK + rows
            inside = jnp.logical_and(position >= starts, position < ends)
            mark = jnp.where(inside, 1.0, 0.0).astype(BF16)
            packed[j] = block
            keys[j] = jnp.where(low, block, mark)
            turned[j] = block.T
            return 0
        return body

    totals[...] = jnp.zeros_like(totals)
    for copy in arrivals:
        copy.wait()
    begin, finish = firsts[0], lasts[-1]
    for part, source in enumerate((prev_ref, own_ref, next_ref)):
        base = part * per_quarter
        lax.fori_loop(
            jnp.maximum(begin, base), jnp.minimum(finish, base + per_quarter), prepare(source, base), 0
        )

    def sweep(first, last, body, carry):
        for step in STEPS:
            groups = (last - first) // step

            def many(t, c, first=first, step=step):
                for u in range(step):
                    c = body(first + t * step + u, c)
                return c

            carry = lax.fori_loop(0, groups, many, carry)
            first = first + groups * step
        return carry

    def query_block(i, _):
        span = pl.ds(pl.multiple_of(i * QUERIES, QUERIES), QUERIES)
        first, last = firsts[0], lasts[0]
        for n in range(1, query_blocks):
            first = jnp.where(i == n, firsts[n], first)
            last = jnp.where(i == n, lasts[n], last)
        qd = qd_ref[span, :]
        position = first_query + i * QUERIES + query_rows
        same = jnp.logical_and(position >= starts, position < ends)
        other = jnp.where(jnp.logical_and(scene_lane, jnp.logical_not(same)), -BARRED, 0.0)
        scaled = qd.astype(F32) * HEAD**-0.5
        query = jnp.where(low, scaled, other).T.astype(BF16)
        nil = jnp.zeros_like(qd)
        only_q = jnp.where(low, scaled.astype(BF16), nil)
        only_d = jnp.where(low, nil, qd)
        pair = jnp.concatenate([only_q, only_d], axis=0)
        grad = only_d.T

        def first_pass(j, top):
            s = dot(keys[j], query)
            scores[j] = s
            return jnp.maximum(top, jnp.max(s.reshape(TOK // 8, 8, QUERIES), axis=0))

        top = sweep(first, last, first_pass, jnp.full((8, QUERIES), -1e30, F32))
        top = jnp.max(top, axis=0, keepdims=True)

        def second_pass(j, carry):
            total, attended = carry
            p = jnp.exp(scores[j] - top)
            total = total + jnp.sum(p.reshape(TOK // 8, 8, QUERIES), axis=0)
            p = p.astype(BF16)
            weights[j] = p
            attended = attended + dot(turned[j, HEAD:, :], p)
            return total, attended

        total, attended = sweep(
            first, last, second_pass, (jnp.zeros((8, QUERIES), F32), jnp.zeros((HEAD, QUERIES), F32))
        )
        share = 1.0 / jnp.sum(total, axis=0, keepdims=True)
        attended = (attended * share).astype(BF16).astype(F32)
        row_dot = jnp.sum(attended * grad[HEAD:, :].astype(F32), axis=0, keepdims=True)

        def third_pass(j, grad_query):
            grad_probs = dot(packed[j], grad)
            probs = weights[j].astype(F32) * share
            grad_scores = (probs * (grad_probs - row_dot)).astype(BF16)
            both = jnp.concatenate([grad_scores, probs.astype(BF16)], axis=1)
            totals[j] += dot(both, pair)
            return grad_query + dot(turned[j, :HEAD, :], grad_scores)

        grad_query = sweep(first, last, third_pass, jnp.zeros((HEAD, QUERIES), F32))
        out = jnp.concatenate([attended, grad_query * HEAD**-0.5], axis=0)
        aq_ref[span, :] = out.T.astype(BF16)
        return 0

    lax.fori_loop(0, query_blocks, query_block, 0)
    leaving = [pltpu.make_async_copy(aq_ref, aq_hbm, left.at[3])]
    leaving[0].start()
    for part, out_hbm in enumerate((kv_prev_hbm, kv_own_hbm, kv_next_hbm)):
        for j in range(per_quarter):
            kv_ref[part, j] = totals[part * per_quarter + j].astype(BF16)
        leaving.append(pltpu.make_async_copy(kv_ref.at[part], out_hbm, left.at[part]))
        leaving[-1].start()
    for copy in leaving:
        copy.wait()


def attention(scene_tiles, place, own, prev, after, qd):
    quarter = own.shape[0]
    blocks = 3 * quarter // TOK
    grads = jax.ShapeDtypeStruct((quarter // TOK, TOK, 2 * HEAD), BF16)
    return pl.pallas_call(
        attention_kernel,
        out_shape=(jax.ShapeDtypeStruct(own.shape, BF16), grads, grads, grads),
        in_specs=[smem(), smem()] + [anywhere()] * 4,
        out_specs=(anywhere(),) * 4,
        scratch_shapes=[pltpu.VMEM(own.shape, BF16)] * 5 + [
            pltpu.VMEM((3, quarter // TOK, TOK, 2 * HEAD), BF16),
            pltpu.SemaphoreType.DMA((4,)),
            pltpu.SemaphoreType.DMA((4,)),
            pltpu.VMEM((blocks, TOK, 2 * HEAD), BF16),
            pltpu.VMEM((blocks, TOK, 2 * HEAD), BF16),
            pltpu.VMEM((blocks, 2 * HEAD, TOK), BF16),
            pltpu.VMEM((blocks, TOK, QUERIES), F32),
            pltpu.VMEM((blocks, TOK, QUERIES), BF16),
            pltpu.VMEM((blocks, TOK, 2 * HEAD), F32),
        ],
        compiler_params=params(),
        name="attention",
    )(scene_tiles, place, own, prev, after, qd)


def finish_kernel(
    core_ref, aq_ref, kv_ref, normed_ref, gout_ref, wqkv_ref, gin_ref, keep_ref, send_ref, att, joint
):
    width = HEADS * HEAD
    for h in range(0, HEADS, 2):
        pair = slice(h * HEAD, (h + 2) * HEAD)
        one, two = aq_ref[h], aq_ref[h + 1]
        att[:, pair] = jnp.concatenate([one[:, :HEAD], two[:, :HEAD]], axis=1)
        joint[:, pair] = jnp.concatenate([one[:, HEAD:], two[:, HEAD:]], axis=1)
        one, two = kv_ref[h], kv_ref[h + 1]
        pair = slice(width + h * HEAD, width + (h + 2) * HEAD)
        joint[:, pair] = jnp.concatenate([one[:, :HEAD], two[:, :HEAD]], axis=1)
        pair = slice(2 * width + h * HEAD, 2 * width + (h + 2) * HEAD)
        joint[:, pair] = jnp.concatenate([one[:, HEAD:], two[:, HEAD:]], axis=1)
    core = core_ref[0]
    grads = joint[...]
    gin_ref[0] = dot(grads, wqkv_ref[...], NT).astype(BF16)
    half = width // 2
    for out_ref, which in ((keep_ref, core), (send_ref, 1 - core)):
        cut = pl.ds(pl.multiple_of(which * half, half), half)
        out_ref[:, : 3 * width] = dot(normed_ref[0, :, cut], grads, TN).astype(BF16)
        out_ref[:, 3 * width :] = dot(att[:, cut], gout_ref[0], TN).astype(BF16)


def finish(core, aq, kv, normed, gout, wqkv):
    width = HEADS * HEAD
    part = jax.ShapeDtypeStruct((width // 2, 4 * width), BF16)
    return pl.pallas_call(
        finish_kernel,
        out_shape=(jax.ShapeDtypeStruct(normed.shape, BF16), part, part),
        in_specs=[smem()] + [vmem()] * 5,
        out_specs=(vmem(),) * 3,
        scratch_shapes=[pltpu.VMEM((TOK, width), BF16), pltpu.VMEM((TOK, 3 * width), BF16)],
        compiler_params=params(),
        name="finish",
    )(core, aq, kv, normed, gout, wqkv)


def pack(kernel, *arrays):
    return pl.pallas_call(
        kernel,
        out_shape=jax.ShapeDtypeStruct((HEADS, TOK, 2 * HEAD), BF16),
        in_specs=[vmem()] * len(arrays),
        out_specs=vmem(),
        compiler_params=params(),
        name="pack",
    )(*arrays)


def spread(x, axes, count):
    return lax.all_to_all(jnp.broadcast_to(x[None], (count,) + x.shape), axes, 0, 0, tiled=True)


def shift(x, by):
    count = lax.axis_size("x")
    return lax.ppermute(x, "x", [(i, i + by) for i in range(count) if 0 <= i + by < count])


def local(normed, query_states, key_states, value_states, grad_output, w_qkv, w_out, scene_tiles):
    heads_axes, seq_axes = ("zl", "y"), ("x", "zl", "y")
    seq_count = lax.axis_size(seq_axes)
    quarter_shape = (lax.axis_size(heads_axes) * TOK, 2 * HEAD)
    place = lax.axis_index("x").reshape(1).astype(jnp.int32)
    core = lax.axis_index("c").reshape(1).astype(jnp.int32)

    def exchange(x):
        return lax.all_to_all(x, heads_axes, 0, 0, tiled=True)

    own = exchange(pack(pack_kv_kernel, key_states, value_states)).reshape(quarter_shape)
    prev, after = shift(own, 1), shift(own, -1)
    qd = exchange(pack(pack_qd_kernel, query_states, grad_output, w_out)).reshape(quarter_shape)
    aq, kv_own, kv_prev, kv_next = attention(scene_tiles, place, own, prev, after, qd)
    from_next, from_prev = shift(kv_prev, -1), shift(kv_next, 1)
    aq = exchange(aq.reshape(HEADS, TOK, 2 * HEAD))
    kv = (kv_own.astype(F32) + from_next.astype(F32) + from_prev.astype(F32)).astype(BF16)
    kv = exchange(kv)
    grad_in, keep, send = finish(core, aq, kv, normed, grad_output, w_qkv)

    swap = [(0, 1), (1, 0)]
    came = lax.ppermute(send, "c", swap)
    part = (keep.astype(F32) + came.astype(F32)).astype(BF16)
    rows, columns = part.shape
    part = part.reshape(seq_count, rows // seq_count, columns)
    part = jnp.sum(lax.all_to_all(part, seq_axes, 0, 0, tiled=True).astype(F32), axis=0)
    part = part.astype(BF16)
    for step in (1, 2):
        partner = [(i, i ^ step) for i in range(lax.axis_size("zh"))]
        part = (part.astype(F32) + lax.ppermute(part, "zh", partner).astype(F32)).astype(BF16)
    mine = spread(part, seq_axes, seq_count).reshape(rows, columns)
    other = lax.ppermute(mine, "c", swap)
    first = core[0] == 0
    total = jnp.concatenate([jnp.where(first, mine, other), jnp.where(first, other, mine)], axis=0)
    total = total.astype(F32)
    joint_width = w_qkv.shape[1]
    return grad_in, total[:, :joint_width], total[:, joint_width:]


def solution(mesh):
    fine = Mesh(mesh.devices.reshape(4, 2, 4, 2, 4), ("zh", "c", "x", "zl", "y"))
    dp, seq = ("zh", "c"), ("x", "zl", "y")
    rows = P(dp, seq, None)
    in_specs = (rows,) * 5 + (P(), P(), P(dp, None))
    return jax.shard_map(local, mesh=fine, in_specs=in_specs, out_specs=(rows, P(), P()), check_vma=False)
```

```python
import jax
import jax.numpy as jnp
from jax import lax
from jax.experimental import pallas as pl
from jax.experimental.pallas import tpu as pltpu
from jax.sharding import Mesh
from jax.sharding import PartitionSpec as P

HEADS = 8
HEAD = 64
TILE = 32
TOK = 256
SCENES = 32
STEPS = (8, 4, 2, 1)
QUERIES = 512
BARRED = 16384.0
F32 = jnp.float32
BF16 = jnp.bfloat16
NT = (((1,), (1,)), ((), ()))
TN = (((0,), (0,)), ((), ()))
VMEM_LIMIT = 48 * 1024 * 1024


def params():
    return pltpu.CompilerParams(vmem_limit_bytes=VMEM_LIMIT)


def vmem():
    return pl.BlockSpec(memory_space=pltpu.VMEM)


def smem():
    return pl.BlockSpec(memory_space=pltpu.SMEM)


def anywhere():
    return pl.BlockSpec(memory_space=pltpu.HBM)


def dot(a, b, dims=(((1,), (0,)), ((), ()))):
    return lax.dot_general(a, b, dims, preferred_element_type=F32)


def pack_two(left, right, out_ref):
    for h in range(HEADS):
        cut = slice(h * HEAD, (h + 1) * HEAD)
        out_ref[h] = jnp.concatenate([left[:, cut], right[:, cut]], axis=1)


def pack_kv_kernel(k_ref, v_ref, out_ref):
    pack_two(k_ref[0], v_ref[0], out_ref)


def pack_qd_kernel(q_ref, g_ref, w_ref, out_ref):
    grad_att = dot(g_ref[0], w_ref[...], NT).astype(BF16)
    pack_two(q_ref[0], grad_att, out_ref)


def attention_kernel(
    tiles_ref, place_ref, own_hbm, prev_hbm, next_hbm, qd_hbm,
    aq_hbm, kv_own_hbm, kv_prev_hbm, kv_next_hbm,
    own_ref, prev_ref, next_ref, qd_ref, aq_ref, kv_ref, came, left,
    packed, keys, turned, scores, weights, totals,
):
    arrivals = [
        pltpu.make_async_copy(source, target, came.at[n])
        for n, (source, target) in enumerate(
            ((own_hbm, own_ref), (qd_hbm, qd_ref), (prev_hbm, prev_ref), (next_hbm, next_ref))
        )
    ]
    for copy in arrivals:
        copy.start()
    quarter = own_ref.shape[0]
    per_quarter = quarter // TOK
    query_blocks = quarter // QUERIES
    first_query = place_ref[0] * quarter
    first_key = first_query - quarter

    lane = lax.broadcasted_iota(jnp.int32, (1, 128), 1)
    low = lane < HEAD

    def read_scenes(s, carry):
        start, starts, ends, lows, highs = carry
        end = start + tiles_ref[0, s] * TILE
        mine = lane == HEAD + s
        starts = jnp.where(mine, start, starts)
        ends = jnp.where(mine, end, ends)
        new_lows, new_highs = [], []
        for i in range(query_blocks):
            head = first_query + i * QUERIES
            tail = head + QUERIES - 1
            new_lows.append(jnp.where(jnp.logical_and(start <= head, head < end), start, lows[i]))
            new_highs.append(jnp.where(jnp.logical_and(start <= tail, tail < end), end, highs[i]))
        return end, starts, ends, tuple(new_lows), tuple(new_highs)

    zero = jnp.int32(0)
    nowhere = jnp.full((1, 128), 2**30, jnp.int32)
    _, starts, ends, lows, highs = lax.fori_loop(
        0, SCENES, read_scenes, (zero, nowhere, nowhere, (zero,) * query_blocks, (zero,) * query_blocks)
    )
    firsts = [(x - first_key) // TOK for x in lows]
    lasts = [(x - first_key + TOK - 1) // TOK for x in highs]

    scene_lane = jnp.logical_and(lane >= HEAD, lane < HEAD + SCENES)
    rows = lax.broadcasted_iota(jnp.int32, (TOK, 1), 0)

    query_rows = lax.broadcasted_iota(jnp.int32, (QUERIES, 1), 0)

    def prepare(source_ref, base):
        def body(j, _):
            block = source_ref[pl.ds(pl.multiple_of((j - base) * TOK, TOK), TOK), :]
            position = first_key + j * TOK + rows
            inside = jnp.logical_and(position >= starts, position < ends)
            mark = jnp.where(inside, 1.0, 0.0).astype(BF16)
            packed[j] = block
            keys[j] = jnp.where(low, block, mark)
            turned[j] = block.T
            return 0
        return body

    totals[...] = jnp.zeros_like(totals)
    for copy in arrivals:
        copy.wait()
    begin, finish = firsts[0], lasts[-1]
    for part, source in enumerate((prev_ref, own_ref, next_ref)):
        base = part * per_quarter
        lax.fori_loop(
            jnp.maximum(begin, base), jnp.minimum(finish, base + per_quarter), prepare(source, base), 0
        )

    def sweep(first, last, body, carry):
        for step in STEPS:
            groups = (last - first) // step

            def many(t, c, first=first, step=step):
                for u in range(step):
                    c = body(first + t * step + u, c)
                return c

            carry = lax.fori_loop(0, groups, many, carry)
            first = first + groups * step
        return carry

    def query_block(i, _):
        span = pl.ds(pl.multiple_of(i * QUERIES, QUERIES), QUERIES)
        first, last = firsts[0], lasts[0]
        for n in range(1, query_blocks):
            first = jnp.where(i == n, firsts[n], first)
            last = jnp.where(i == n, lasts[n], last)
        qd = qd_ref[span, :]
        position = first_query + i * QUERIES + query_rows
        same = jnp.logical_and(position >= starts, position < ends)
        other = jnp.where(jnp.logical_and(scene_lane, jnp.logical_not(same)), -BARRED, 0.0)
        scaled = qd.astype(F32) * HEAD**-0.5
        query = jnp.where(low, scaled, other).T.astype(BF16)
        nil = jnp.zeros_like(qd)
        only_q = jnp.where(low, scaled.astype(BF16), nil)
        only_d = jnp.where(low, nil, qd)
        pair = jnp.concatenate([only_q, only_d], axis=0)
        grad = only_d.T

        def first_pass(j, top):
            s = dot(keys[j], query)
            scores[j] = s
            return jnp.maximum(top, jnp.max(s.reshape(TOK // 8, 8, QUERIES), axis=0))

        top = sweep(first, last, first_pass, jnp.full((8, QUERIES), -1e30, F32))
        top = jnp.max(top, axis=0, keepdims=True)

        def second_pass(j, carry):
            total, attended = carry
            p = jnp.exp(scores[j] - top)
            total = total + jnp.sum(p.reshape(TOK // 8, 8, QUERIES), axis=0)
            p = p.astype(BF16)
            weights[j] = p
            attended = attended + dot(turned[j, HEAD:, :], p)
            return total, attended

        total, attended = sweep(
            first, last, second_pass, (jnp.zeros((8, QUERIES), F32), jnp.zeros((HEAD, QUERIES), F32))
        )
        share = 1.0 / jnp.sum(total, axis=0, keepdims=True)
        attended = (attended * share).astype(BF16).astype(F32)
        row_dot = jnp.sum(attended * grad[HEAD:, :].astype(F32), axis=0, keepdims=True)

        def third_pass(j, grad_query):
            grad_probs = dot(packed[j], grad)
            probs = weights[j].astype(F32) * share
            grad_scores = (probs * (grad_probs - row_dot)).astype(BF16)
            both = jnp.concatenate([grad_scores, probs.astype(BF16)], axis=1)
            totals[j] += dot(both, pair)
            return grad_query + dot(turned[j, :HEAD, :], grad_scores)

        grad_query = sweep(first, last, third_pass, jnp.zeros((HEAD, QUERIES), F32))
        out = jnp.concatenate([attended, grad_query * HEAD**-0.5], axis=0)
        aq_ref[span, :] = out.T.astype(BF16)
        return 0

    lax.fori_loop(0, query_blocks, query_block, 0)
    leaving = [pltpu.make_async_copy(aq_ref, aq_hbm, left.at[3])]
    leaving[0].start()
    for part, out_hbm in enumerate((kv_prev_hbm, kv_own_hbm, kv_next_hbm)):
        for j in range(per_quarter):
            kv_ref[part, j] = totals[part * per_quarter + j].astype(BF16)
        leaving.append(pltpu.make_async_copy(kv_ref.at[part], out_hbm, left.at[part]))
        leaving[-1].start()
    for copy in leaving:
        copy.wait()


def attention(scene_tiles, place, own, prev, after, qd):
    quarter = own.shape[0]
    blocks = 3 * quarter // TOK
    grads = jax.ShapeDtypeStruct((quarter // TOK, TOK, 2 * HEAD), BF16)
    return pl.pallas_call(
        attention_kernel,
        out_shape=(jax.ShapeDtypeStruct(own.shape, BF16), grads, grads, grads),
        in_specs=[smem(), smem()] + [anywhere()] * 4,
        out_specs=(anywhere(),) * 4,
        scratch_shapes=[pltpu.VMEM(own.shape, BF16)] * 5 + [
            pltpu.VMEM((3, quarter // TOK, TOK, 2 * HEAD), BF16),
            pltpu.SemaphoreType.DMA((4,)),
            pltpu.SemaphoreType.DMA((4,)),
            pltpu.VMEM((blocks, TOK, 2 * HEAD), BF16),
            pltpu.VMEM((blocks, TOK, 2 * HEAD), BF16),
            pltpu.VMEM((blocks, 2 * HEAD, TOK), BF16),
            pltpu.VMEM((blocks, TOK, QUERIES), F32),
            pltpu.VMEM((blocks, TOK, QUERIES), BF16),
            pltpu.VMEM((blocks, TOK, 2 * HEAD), F32),
        ],
        compiler_params=params(),
        name="attention",
    )(scene_tiles, place, own, prev, after, qd)


def finish_kernel(
    core_ref, aq_ref, kv_ref, normed_ref, gout_ref, wqkv_ref, gin_ref, keep_ref, send_ref, att, joint
):
    width = HEADS * HEAD
    for h in range(0, HEADS, 2):
        pair = slice(h * HEAD, (h + 2) * HEAD)
        one, two = aq_ref[h], aq_ref[h + 1]
        att[:, pair] = jnp.concatenate([one[:, :HEAD], two[:, :HEAD]], axis=1)
        joint[:, pair] = jnp.concatenate([one[:, HEAD:], two[:, HEAD:]], axis=1)
        one, two = kv_ref[h], kv_ref[h + 1]
        pair = slice(width + h * HEAD, width + (h + 2) * HEAD)
        joint[:, pair] = jnp.concatenate([one[:, :HEAD], two[:, :HEAD]], axis=1)
        pair = slice(2 * width + h * HEAD, 2 * width + (h + 2) * HEAD)
        joint[:, pair] = jnp.concatenate([one[:, HEAD:], two[:, HEAD:]], axis=1)
    core = core_ref[0]
    grads = joint[...]
    gin_ref[0] = dot(grads, wqkv_ref[...], NT).astype(BF16)
    half = width // 2
    for out_ref, which in ((keep_ref, core), (send_ref, 1 - core)):
        cut = pl.ds(pl.multiple_of(which * half, half), half)
        out_ref[:, : 3 * width] = dot(normed_ref[0, :, cut], grads, TN).astype(BF16)
        out_ref[:, 3 * width :] = dot(att[:, cut], gout_ref[0], TN).astype(BF16)


def finish(core, aq, kv, normed, gout, wqkv):
    width = HEADS * HEAD
    part = jax.ShapeDtypeStruct((width // 2, 4 * width), BF16)
    return pl.pallas_call(
        finish_kernel,
        out_shape=(jax.ShapeDtypeStruct(normed.shape, BF16), part, part),
        in_specs=[smem()] + [vmem()] * 5,
        out_specs=(vmem(),) * 3,
        scratch_shapes=[pltpu.VMEM((TOK, width), BF16), pltpu.VMEM((TOK, 3 * width), BF16)],
        compiler_params=params(),
        name="finish",
    )(core, aq, kv, normed, gout, wqkv)


def pack(kernel, *arrays):
    return pl.pallas_call(
        kernel,
        out_shape=jax.ShapeDtypeStruct((HEADS, TOK, 2 * HEAD), BF16),
        in_specs=[vmem()] * len(arrays),
        out_specs=vmem(),
        compiler_params=params(),
        name="pack",
    )(*arrays)


def place_kernel(core_ref, mine_ref, other_ref, qkv_ref, out_ref):
    rows = mine_ref.shape[0]
    split = qkv_ref.shape[1]

    def lay(*halves):
        for n, ref in enumerate(halves):
            spot = slice(n * rows, (n + 1) * rows)
            qkv_ref[spot, :] = ref[:, :split].astype(F32)
            out_ref[spot, :] = ref[:, split:].astype(F32)

    pl.when(core_ref[0] == 0)(lambda: lay(mine_ref, other_ref))
    pl.when(core_ref[0] != 0)(lambda: lay(other_ref, mine_ref))


def place_sums(core, mine, other):
    width = HEADS * HEAD
    return pl.pallas_call(
        place_kernel,
        out_shape=(
            jax.ShapeDtypeStruct((width, 3 * width), F32),
            jax.ShapeDtypeStruct((width, width), F32),
        ),
        in_specs=[smem()] + [vmem()] * 2,
        out_specs=(vmem(),) * 2,
        compiler_params=params(),
        name="place_sums",
    )(core, mine, other)


def spread(x, axes, count):
    return lax.all_to_all(jnp.broadcast_to(x[None], (count,) + x.shape), axes, 0, 0, tiled=True)


def shift(x, by):
    count = lax.axis_size("x")
    return lax.ppermute(x, "x", [(i, i + by) for i in range(count) if 0 <= i + by < count])


def local(normed, query_states, key_states, value_states, grad_output, w_qkv, w_out, scene_tiles):
    heads_axes, seq_axes = ("zl", "y"), ("x", "zl", "y")
    seq_count = lax.axis_size(seq_axes)
    quarter_shape = (lax.axis_size(heads_axes) * TOK, 2 * HEAD)
    place = lax.axis_index("x").reshape(1).astype(jnp.int32)
    core = lax.axis_index("c").reshape(1).astype(jnp.int32)

    def exchange(x):
        return lax.all_to_all(x, heads_axes, 0, 0, tiled=True)

    own = exchange(pack(pack_kv_kernel, key_states, value_states)).reshape(quarter_shape)
    prev, after = shift(own, 1), shift(own, -1)
    qd = exchange(pack(pack_qd_kernel, query_states, grad_output, w_out)).reshape(quarter_shape)
    aq, kv_own, kv_prev, kv_next = attention(scene_tiles, place, own, prev, after, qd)
    from_next, from_prev = shift(kv_prev, -1), shift(kv_next, 1)
    aq = exchange(aq.reshape(HEADS, TOK, 2 * HEAD))
    kv = (kv_own.astype(F32) + from_next.astype(F32) + from_prev.astype(F32)).astype(BF16)
    kv = exchange(kv)
    grad_in, keep, send = finish(core, aq, kv, normed, grad_output, w_qkv)

    swap = [(0, 1), (1, 0)]
    came = lax.ppermute(send, "c", swap)
    part = (keep.astype(F32) + came.astype(F32)).astype(BF16)
    rows, columns = part.shape
    part = part.reshape(seq_count, rows // seq_count, columns)
    part = jnp.sum(lax.all_to_all(part, seq_axes, 0, 0, tiled=True).astype(F32), axis=0)
    part = part.astype(BF16)
    for step in (1, 2):
        partner = [(i, i ^ step) for i in range(lax.axis_size("zh"))]
        part = (part.astype(F32) + lax.ppermute(part, "zh", partner).astype(F32)).astype(BF16)
    mine = spread(part, seq_axes, seq_count).reshape(rows, columns)
    other = lax.ppermute(mine, "c", swap)
    total_qkv, total_out = place_sums(core, mine, other)
    return grad_in, total_qkv, total_out


def solution(mesh):
    fine = Mesh(mesh.devices.reshape(4, 2, 4, 2, 4), ("zh", "c", "x", "zl", "y"))
    dp, seq = ("zh", "c"), ("x", "zl", "y")
    rows = P(dp, seq, None)
    in_specs = (rows,) * 5 + (P(), P(), P(dp, None))
    return jax.shard_map(local, mesh=fine, in_specs=in_specs, out_specs=(rows, P(), P()), check_vma=False)
```
